32 devices in a mesh: dp: 4 (over z), ctx: 4 (over y, core), tp: 2 (over x).
Axes of the slice: x: 2, y: 2, z: 4, core: 2. Of those that a mesh axis runs over, the one named last changes fastest.
Arguments:
- tokens: bfloat16 [4, 4096, 1024], P('dp', 'ctx'), may hold values from -6 to 6
- lengths: int32 [4], replicated, may hold values from 1 to 1024, as said below
- norm_gain: bfloat16 [2, 1024], P(None, ('dp', 'ctx')), may hold values from 0.25 to 1.75
- norm_bias: bfloat16 [2, 1024], P(None, ('dp', 'ctx')), may hold values from -1.5 to 1.5
- qkv_weight: bfloat16 [1024, 3, 1024], P(('dp', 'ctx'), None, 'tp'), may hold values from -0.1875 to 0.1875
- qv_bias: float32 [2, 1024], P(None, 'tp'), may hold values from -1.5 to 1.5
- out_weight: bfloat16 [1024, 1024], P('tp', ('dp', 'ctx')), may hold values from -2.5 to 2.5
- mlp_in: bfloat16 [1024, 4096], P(('dp', 'ctx'), 'tp'), may hold values from -0.1875 to 0.1875
- mlp_bias: float32 [4096], P('tp'), may hold values from -1.5 to 1.5
- mlp_out: bfloat16 [4096, 1024], P('tp', ('dp', 'ctx')), may hold values from -0.125 to 0.125
- out_bias: bfloat16 [2, 1024], P(None, ('dp', 'ctx')), may hold values from -1.5 to 1.5
- cotangent: bfloat16 [4, 4096, 1024], P('dp', 'ctx'), may hold values from -6 to 6
Outputs:
- result: bfloat16 [4, 4096, 1024], P('dp', 'ctx')
- grad_tokens: bfloat16 [4, 4096, 1024], P('dp', 'ctx')
- grad_norm_gain: float32 [2, 1024], P(None, ('dp', 'ctx'))
- grad_norm_bias: float32 [2, 1024], P(None, ('dp', 'ctx'))
- grad_qkv_weight: float32 [1024, 3, 1024], P(('dp', 'ctx'), None, 'tp')
- grad_qv_bias: float32 [2, 1024], P(None, 'tp')
- grad_out_weight: float32 [1024, 1024], P('tp', ('dp', 'ctx'))
- grad_mlp_in: float32 [1024, 4096], P(('dp', 'ctx'), 'tp')
- grad_mlp_bias: float32 [4096], P('tp')
- grad_mlp_out: float32 [4096, 1024], P('tp', ('dp', 'ctx'))
- grad_out_bias: float32 [2, 1024], P(None, ('dp', 'ctx'))
The draws below stay inside these ranges and needn't reach their ends.
Inputs may be any that keep to these rules, and one draw needn't show every extreme that they name: `lengths`: entry c counts the live tokens at the start of context device c's block of 1024 slots of every image; the entries sum to 3072, every entry is at least 1, and exactly one entry is 1024.
All inputs are finite; a program needn't handle non-finite values.
Results may differ from the reference program's by a relative error of at most 0.02.
Values may be sent and summed in bfloat16 or wider, within the bound.
No kernel may reach another device: no remote copies, remote signals or barrier semaphores. Data moves between devices by JAX's collectives and lax.ppermute only.
A program may use at most 384 MiB of HBM per device.

```python
import jax
import jax.numpy as jnp
from jax import lax

D = 1024
HEADS = 16
HD = 64
FF = 4096
CAP = 1024
IMAGES = 4
SLOTS = 4096
SEQ = 3072
N_CTX = 4


def draw_lengths(key, part):
    key = jax.random.fold_in(key, 11)
    place_key, move_key = jax.random.split(key)
    others_count = N_CTX - 1
    remaining = SEQ - CAP
    share = remaining // others_count
    extra = remaining - share * others_count
    spread = max(0, min(share - 1, CAP - share - 1) // 2)
    index_others = jnp.arange(others_count, dtype=jnp.int32)
    others = jnp.full((others_count,), share, jnp.int32) + (index_others < extra).astype(jnp.int32)
    moves = jax.random.randint(move_key, (others_count,), -spread, spread + 1, dtype=jnp.int32)
    others = others + moves - jnp.roll(moves, 1)
    full_place = jax.random.randint(place_key, (), 0, N_CTX, dtype=jnp.int32)
    index_all = jnp.arange(N_CTX, dtype=jnp.int32)
    source = jnp.clip(index_all - (index_all > full_place).astype(jnp.int32), 0, others_count - 1)
    return jnp.where(index_all == full_place, CAP, others[source]).astype(jnp.int32)


def block_scale(rng, dims, shards, least, high):
    level, own = 1.0, jax.random.fold_in(rng, 6)
    for position, blocks in shards:
        draws = jnp.exp(jax.random.uniform(jax.random.fold_in(own, position), (blocks,), jnp.float32, least / len(shards), high / len(shards)))
        level = level * jnp.repeat(draws, dims[position] // blocks).reshape([-1 if axis == position else 1 for axis in range(len(dims))])
    return level


def bell_draw(key, shape, deviation, reach, pieces=(), kind=jnp.bfloat16):
    factor_of = block_scale(key, shape, pieces, -0.22, 0.18) if pieces else 1.0
    drawn = jax.random.normal(key, shape, jnp.float32) * deviation * factor_of
    return jnp.minimum(jnp.maximum(drawn, -reach), reach).astype(kind)


def setup_inputs(seed: int = 0) -> dict:
    arg_keys = jax.random.split(jax.random.key(seed), 13)
    return {
        "tokens": bell_draw(arg_keys[0], (IMAGES, SLOTS, D), 1.0, 6.0, ((0, 4), (1, 4))),
        "lengths": draw_lengths(jax.random.fold_in(arg_keys[12], 71), 0),
        "norm_gain": jnp.clip(1.0 + 0.15 * jax.random.normal(arg_keys[2], (2, D), jnp.float32), 0.25, 1.75).astype(jnp.bfloat16),
        "norm_bias": bell_draw(arg_keys[3], (2, D), 0.3, 1.5, ((1, 16),)),
        "qkv_weight": bell_draw(arg_keys[4], (D, 3, D), D ** -0.5, 0.1875, ((0, 16), (2, 2))),
        "qv_bias": bell_draw(arg_keys[5], (2, D), 0.3, 1.5, ((1, 2),), jnp.float32),
        "out_weight": bell_draw(arg_keys[6], (D, D), (max(D * 16 // SEQ, 1)) ** -0.5, 2.5, ((0, 2), (1, 16))),
        "mlp_in": bell_draw(arg_keys[7], (D, FF), D ** -0.5, 0.1875, ((0, 16), (1, 2))),
        "mlp_bias": bell_draw(arg_keys[8], (FF,), 0.3, 1.5, ((0, 2),), jnp.float32),
        "mlp_out": bell_draw(arg_keys[9], (FF, D), (FF // 2) ** -0.5, 0.125, ((0, 2), (1, 16))),
        "out_bias": bell_draw(arg_keys[10], (2, D), 0.3, 1.5, ((1, 16),)),
        "cotangent": bell_draw(arg_keys[11], (IMAGES, SLOTS, D), 1.0, 6.0, ((0, 4), (1, 4))),
    }


@jax.custom_vjp
def low(v):
    return lax.optimization_barrier(v.astype(jnp.bfloat16)).astype(jnp.float32)

@jax.custom_vjp
def low_back(v):
    return v

def low_keep(v):
    return (low(v), None)

def low_pass(kept, grad):
    return (grad,)

def back_keep(v):
    return (v, None)

def back_low(kept, grad):
    return (low(grad),)
low.defvjp(low_keep, low_pass)
low_back.defvjp(back_keep, back_low)
NEG = -1e+30
EPS = 1e-06

def mult(form, left, right):
    return jnp.einsum(form, left, right, precision=lax.Precision.HIGHEST)

def normalize(values, gain, shift):
    mean = lax.optimization_barrier(jnp.mean(values, axis=-1, keepdims=True))
    centred = values - mean
    var = lax.optimization_barrier(jnp.mean(centred * centred, axis=-1, keepdims=True))
    return centred * lax.rsqrt(var + EPS) * gain + shift

def reference(tokens, lengths, norm_gain, norm_bias, qkv_weight, qv_bias, out_weight, mlp_in, mlp_bias, mlp_out, out_bias, cotangent):
    positions = jnp.arange(SLOTS, dtype=jnp.int32)
    limit = jnp.take(lengths, positions // CAP)
    live = positions % CAP < limit
    live_col = live.astype(jnp.float32)[:, None]
    factor = 1.0 / HD ** 0.5

    def forward(x_all, gains, shifts, w_qkv, qv, w_out, w_in, b_in, w_down, b_out):

        def one_image(x):
            h1 = low(normalize(x, gains[0], shifts[0]))
            qkv = mult('td,dke->tke', h1, w_qkv)
            query = low_back(low(qkv[:, 0] + qv[0])).reshape(SLOTS, HEADS, HD)
            key = low_back(low(qkv[:, 1])).reshape(SLOTS, HEADS, HD)
            value = low_back(low(qkv[:, 2] + qv[1])).reshape(SLOTS, HEADS, HD)

            def block(query_block):
                score = mult('qhd,khd->hqk', query_block, key) * factor
                score = low_back(score)
                score = jnp.where(live[None, None, :], score, NEG)
                top = lax.optimization_barrier(jnp.max(score, axis=-1, keepdims=True))
                expo = jnp.where(live[None, None, :], jnp.exp(score - top), 0.0)
                prob = low(expo / lax.optimization_barrier(jnp.sum(expo, axis=-1, keepdims=True)))
                return mult('hqk,khd->qhd', prob, value)
            blocks = query.reshape(SLOTS // CAP, CAP, HEADS, HD)
            attended = lax.map(jax.checkpoint(block), blocks).reshape(SLOTS, D)
            attended = low_back(low(attended))
            branch = low_back(mult('te,ed->td', attended, w_out) + b_out[0])
            x1 = x + branch
            h2 = low(normalize(x1, gains[1], shifts[1]))
            pre = low_back(mult('td,df->tf', h2, w_in) + b_in)
            act = low(jax.nn.gelu(pre, approximate=False))
            down = low_back(mult('tf,fd->td', act, w_down) + b_out[1])
            return (x1 + down) * live_col
        return lax.map(jax.checkpoint(one_image), x_all)
    params = tuple((a.astype(jnp.float32) for a in (norm_gain, norm_bias, qkv_weight, qv_bias, out_weight, mlp_in, mlp_bias, mlp_out, out_bias)))
    result, back = jax.vjp(forward, tokens.astype(jnp.float32), *params)
    grads = back(cotangent.astype(jnp.float32))
    return (result.astype(jnp.bfloat16), grads[0].astype(jnp.bfloat16), grads[1], grads[2], grads[3], grads[4], grads[5], grads[6], grads[7], grads[8], grads[9])
```

```python
import functools
import math

import jax
import jax.numpy as jnp
from jax import lax
from jax.experimental import pallas as pl
from jax.experimental.pallas import tpu as pltpu
from jax.sharding import PartitionSpec as P

HD = 64
PAIR = 2 * HD
EPS = 1e-06
LOG2E = 1.4426950408889634
BF = jnp.bfloat16
F32 = jnp.float32
VMEM_LIMIT = 56 * 1024 * 1024
PAIRS_PER_CALL = 1
KEY_TILE = 512
QUERY_TILE = 256
HIDDEN_TILE = 256


def dot_nt(a, b):
    return lax.dot_general(a, b, (((1,), (1,)), ((), ())), preferred_element_type=F32)


def dot_tn(a, b):
    return lax.dot_general(a, b, (((0,), (0,)), ((), ())), preferred_element_type=F32)


def dot_nn(a, b):
    return jnp.dot(a, b, preferred_element_type=F32)


def swap_core(v):
    return lax.ppermute(v, "ctx", [(0, 1), (1, 0), (2, 3), (3, 2)])


def swap_y(v):
    return lax.ppermute(v, "ctx", [(0, 2), (2, 0), (1, 3), (3, 1)])


def gather_ctx(v):
    over = swap_y(v)
    return v, swap_core(v), over, swap_core(over)


def sum_tp(part):
    if lax.axis_size("tp") == 2:
        other = lax.ppermute(part, "tp", [(0, 1), (1, 0)])
        return part.astype(F32) + other.astype(F32)
    return lax.psum(part, "tp").astype(F32)


def gather_line(v):
    n = lax.axis_size("dp")
    z = lax.axis_index("dp")
    from_low, from_high = [], []
    up = down = v
    for _ in range(n - 1):
        up = lax.ppermute(up, "dp", [(i, i + 1) for i in range(n - 1)])
        down = lax.ppermute(down, "dp", [(i + 1, i) for i in range(n - 1)])
        from_low.append(up)
        from_high.append(down)
    held = jnp.stack(from_low[::-1] + [v] + from_high)
    return lax.dynamic_slice_in_dim(held, n - 1 - z, n, 0)


def gather_rows(shard):
    me = lax.axis_index("ctx")
    odd_core, odd_y = (me & 1) == 1, (me >> 1) == 1
    b0, b1, b2, b3 = gather_ctx(gather_line(shard))
    lo, hi = jnp.where(odd_core, b1, b0), jnp.where(odd_core, b0, b1)
    lo_far, hi_far = jnp.where(odd_core, b3, b2), jnp.where(odd_core, b2, b3)
    whole = jnp.stack(
        [
            jnp.where(odd_y, lo_far, lo),
            jnp.where(odd_y, hi_far, hi),
            jnp.where(odd_y, lo, lo_far),
            jnp.where(odd_y, hi, hi_far),
        ],
        axis=1,
    )
    return whole.reshape(-1, shard.shape[1])


def scatter_line(v):
    n = lax.axis_size("dp")
    z = lax.axis_index("dp")

    def at(i):
        return lax.dynamic_index_in_dim(v, jnp.clip(i, 0, n - 1), 0, keepdims=False)

    up, down = at(z + n - 1), at(z - n + 1)
    for step in range(1, n):
        up = lax.ppermute(up, "dp", [(i, i + 1) for i in range(n - 1)])
        down = lax.ppermute(down, "dp", [(i + 1, i) for i in range(n - 1)])
        if step < n - 1:
            up = (up.astype(F32) + at(z + n - 1 - step).astype(F32)).astype(BF)
            down = (down.astype(F32) + at(z - n + 1 + step).astype(F32)).astype(BF)
    return at(z).astype(F32) + up.astype(F32) + down.astype(F32)


def scatter_rows(v):
    n = lax.axis_size("dp")
    me = lax.axis_index("ctx")
    core, y = me & 1, me >> 1
    rows, columns = v.shape
    v = v.reshape(n, 2, 2, rows // (4 * n), columns)

    def pick(a, i, axis):
        return lax.dynamic_index_in_dim(a, i, axis, keepdims=False)

    v = (pick(v, core, 2).astype(F32) + swap_core(pick(v, 1 - core, 2)).astype(F32)).astype(BF)
    v = (pick(v, y, 1).astype(F32) + swap_y(pick(v, 1 - y, 1)).astype(F32)).astype(BF)
    return scatter_line(v)


def sum_small(v):
    n = lax.axis_size("dp")
    v = v + swap_core(v)
    v = v + swap_y(v)
    bit = 1
    while bit < n:
        v = v + lax.ppermute(v, "dp", [(i, i ^ bit) for i in range(n)])
        bit *= 2
    return v


def attend_kernel(scale, q_ref, k0, k1, k2, k3, o_ref, lse_ref):
    rows = q_ref.shape[0]
    tile = min(QUERY_TILE, rows)
    first = lax.broadcasted_iota(jnp.int32, (1, PAIR), 1) < HD

    def step(i, carry):
        at = pl.ds(pl.multiple_of(i * tile, tile), tile)
        q = q_ref[at, :]
        outs = []
        for h in range(2):
            mine = first if h == 0 else jnp.logical_not(first)
            q_h = jnp.where(mine, q, jnp.zeros_like(q))
            scores = [dot_nt(q_h, k[:, :PAIR]) for k in (k0, k1, k2, k3)]
            top = functools.reduce(
                jnp.maximum, [jnp.max(s, axis=1, keepdims=True) for s in scores]
            )
            acc = None
            for s, k in zip(scores, (k0, k1, k2, k3)):
                p = jnp.exp2((s - top) * scale).astype(BF)
                v = k[:, PAIR:]
                term = dot_nn(p, jnp.where(mine, v, jnp.ones_like(v)))
                acc = term if acc is None else acc + term
            total = pltpu.roll(acc, HD, 1)
            outs.append(acc / total)
            lse = jnp.transpose(top * scale + jnp.log2(total))
            lse_ref[0, pl.ds(h, 1), at] = lse[h * HD : h * HD + 1, :]
        o_ref[at, :] = jnp.where(first, outs[0], outs[1])
        return carry

    lax.fori_loop(0, rows // tile, step, 0)


def attend(q, blocks, call):
    rows = q.shape[0]
    width = blocks[0].shape[1] // 2
    pairs = width // PAIR
    base = call * pairs
    keys = 4 * rows
    kv_spec = pl.BlockSpec((rows, 2 * PAIR), lambda i: (0, i))
    return pl.pallas_call(
        functools.partial(attend_kernel, LOG2E / math.sqrt(HD)),
        grid=(pairs,),
        in_specs=[pl.BlockSpec((rows, PAIR), lambda i: (0, base + i))] + [kv_spec] * 4,
        out_specs=[
            pl.BlockSpec((rows, PAIR), lambda i: (0, i)),
            pl.BlockSpec((1, 8, rows), lambda i: (i, 0, 0)),
        ],
        out_shape=[
            jax.ShapeDtypeStruct((rows, width), F32),
            jax.ShapeDtypeStruct((pairs, 8, rows), F32),
        ],
        cost_estimate=pl.CostEstimate(
            flops=16 * rows * keys * width,
            bytes_accessed=rows * width * 16,
            transcendentals=rows * keys * width // HD,
        ),
        compiler_params=pltpu.CompilerParams(vmem_limit_bytes=VMEM_LIMIT),
        name="attend",
    )(q, *blocks)


def attend_back_kernel(
    scale, factor, q_ref, d_ref, o_ref, lse_ref, k0, k1, k2, k3,
    dq_ref, keep_ref, send_ref, kv, dkv, dq_turned,
):
    rows = q_ref.shape[0]
    keys = 4 * rows
    tile = min(KEY_TILE, rows)
    for place, block in enumerate((k0, k2, k1, k3)):
        kv[place * rows : (place + 1) * rows, :] = block[...]
    first = lax.broadcasted_iota(jnp.int32, (1, PAIR), 1) < HD
    d = d_ref[...]
    q = q_ref[...]
    prod = jnp.transpose(d.astype(F32) * o_ref[...])
    halves = []
    for h in range(2):
        mine = first if h == 0 else jnp.logical_not(first)
        halves.append((
            jnp.where(mine, q, jnp.zeros_like(q)),
            jnp.where(mine, d, jnp.zeros_like(d)),
            lse_ref[0, h : h + 1, :],
            jnp.sum(prod[h * HD : (h + 1) * HD, :], axis=0, keepdims=True),
        ))
    dq_turned[...] = jnp.zeros_like(dq_turned)

    def step(i, carry):
        at = pl.ds(pl.multiple_of(i * tile, tile), tile)
        k = kv[at, :PAIR]
        v = kv[at, PAIR:]
        k_turned = jnp.transpose(k)
        dk = dv = None
        for h, (q_h, d_h, lse, delta) in enumerate(halves):
            prob = jnp.exp2(dot_nt(k, q_h) * scale - lse)
            d_score = (prob * (dot_nt(v, d_h) - delta)).astype(BF)
            dv_h = dot_nn(prob.astype(BF), d_h)
            dk_h = dot_nn(d_score, q_h)
            dv = dv_h if dv is None else dv + dv_h
            dk = dk_h if dk is None else dk + dk_h
            part = slice(h * HD, (h + 1) * HD)
            dq_turned[part, :] += dot_nn(k_turned[part, :], d_score)
        dkv[at, :PAIR] = (dk * factor).astype(BF)
        dkv[at, PAIR:] = dv.astype(BF)
        return carry

    lax.fori_loop(0, keys // tile, step, 0)
    dq_ref[...] = (jnp.transpose(dq_turned[...]) * factor).astype(BF)
    keep_ref[...] = dkv[: 2 * rows, :]
    send_ref[...] = dkv[2 * rows :, :]


def attend_back(q, d_att, o, lse, blocks, call):
    rows = q.shape[0]
    width = blocks[0].shape[1] // 2
    pairs = width // PAIR
    base = call * pairs
    keys = 4 * rows
    kv_spec = pl.BlockSpec((rows, 2 * PAIR), lambda i: (0, i))
    wide = pl.BlockSpec((rows, PAIR), lambda i: (0, base + i))
    narrow = pl.BlockSpec((rows, PAIR), lambda i: (0, i))
    twice = pl.BlockSpec((2 * rows, 2 * PAIR), lambda i: (0, i))
    return pl.pallas_call(
        functools.partial(attend_back_kernel, LOG2E / math.sqrt(HD), 1.0 / math.sqrt(HD)),
        grid=(pairs,),
        in_specs=[wide, wide, narrow, pl.BlockSpec((1, 8, rows), lambda i: (i, 0, 0))]
        + [kv_spec] * 4,
        out_specs=[narrow, twice, twice],
        out_shape=[
            jax.ShapeDtypeStruct((rows, width), BF),
            jax.ShapeDtypeStruct((2 * rows, 2 * width), BF),
            jax.ShapeDtypeStruct((2 * rows, 2 * width), BF),
        ],
        scratch_shapes=[
            pltpu.VMEM((keys, 2 * PAIR), BF),
            pltpu.VMEM((keys, 2 * PAIR), BF),
            pltpu.VMEM((PAIR, rows), F32),
        ],
        cost_estimate=pl.CostEstimate(
            flops=40 * rows * keys * width,
            bytes_accessed=rows * width * 40,
            transcendentals=rows * keys * width // HD,
        ),
        compiler_params=pltpu.CompilerParams(vmem_limit_bytes=VMEM_LIMIT),
        name="attend_back",
    )(q, d_att, o, lse, *blocks)


def mlp_kernel(
    h2_ref, d_ref, in_ref, down_ref, bias_ref,
    act_ref, dpre_ref, y_ref, back_ref, bias_grad_ref, y_acc, back_acc,
):
    i = pl.program_id(0)
    w_in, w_down = in_ref[...], down_ref[...]
    pre = dot_nn(h2_ref[...], w_in) + bias_ref[...]
    d_act = dot_nn(d_ref[...], w_down)
    below = 0.5 * (1.0 + lax.erf(pre * math.sqrt(0.5)))
    act = (pre * below).astype(BF)
    slope = below + pre * (jnp.exp(-0.5 * pre * pre) * (1.0 / math.sqrt(2.0 * math.pi)))
    d_pre = (d_act * slope).astype(BF)
    act_ref[...] = act
    dpre_ref[...] = d_pre
    bias_grad_ref[...] = jnp.sum(d_pre.astype(F32), axis=0, keepdims=True)
    y = dot_nt(act, w_down)
    back = dot_nt(d_pre, w_in)

    @pl.when(i == 0)
    def _():
        y_acc[...] = y
        back_acc[...] = back

    @pl.when(i > 0)
    def _():
        y_acc[...] += y
        back_acc[...] += back

    @pl.when(i == pl.num_programs(0) - 1)
    def _():
        y_ref[...] = y_acc[...].astype(BF)
        back_ref[...] = back_acc[...].astype(BF)


def mlp(h2, d_down, w_in, w_down, bias):
    rows, width = h2.shape
    hidden = w_in.shape[1]
    tile = min(HIDDEN_TILE, hidden)
    held = pl.BlockSpec((rows, width), lambda i: (0, 0))
    weight = pl.BlockSpec((width, tile), lambda i: (0, i))
    out = pl.BlockSpec((rows, tile), lambda i: (0, i))
    line = pl.BlockSpec((1, tile), lambda i: (0, i))
    return pl.pallas_call(
        mlp_kernel,
        grid=(hidden // tile,),
        in_specs=[held, held, weight, weight, line],
        out_specs=[out, out, held, held, line],
        out_shape=[
            jax.ShapeDtypeStruct((rows, hidden), BF),
            jax.ShapeDtypeStruct((rows, hidden), BF),
            jax.ShapeDtypeStruct((rows, width), BF),
            jax.ShapeDtypeStruct((rows, width), BF),
            jax.ShapeDtypeStruct((1, hidden), F32),
        ],
        scratch_shapes=[pltpu.VMEM((rows, width), F32), pltpu.VMEM((rows, width), F32)],
        cost_estimate=pl.CostEstimate(
            flops=8 * rows * width * hidden,
            bytes_accessed=4 * width * hidden + 4 * rows * hidden + 8 * rows * width,
            transcendentals=rows * hidden,
        ),
        compiler_params=pltpu.CompilerParams(vmem_limit_bytes=VMEM_LIMIT),
        name="mlp",
    )(h2, d_down, w_in, w_down, bias)


def norm_parts(v):
    mean = jnp.mean(v, axis=-1, keepdims=True)
    centred = v - mean
    var = jnp.mean(centred * centred, axis=-1, keepdims=True)
    rstd = lax.rsqrt(var + EPS)
    return centred * rstd, rstd


def norm_back(d, unit, rstd, gain):
    d_unit = d * gain
    return rstd * (
        d_unit
        - jnp.mean(d_unit, axis=-1, keepdims=True)
        - unit * jnp.mean(d_unit * unit, axis=-1, keepdims=True)
    )


def body(
    tokens,
    lengths,
    norm_gain,
    norm_bias,
    qkv_weight,
    qv_bias,
    out_weight,
    mlp_in,
    mlp_bias,
    mlp_out,
    out_bias,
    cotangent,
):
    _, cap, width = tokens.shape
    n_ctx = lax.axis_size("ctx")
    slots = n_ctx * cap
    rows = 3 * slots // 4 // n_ctx
    spare = cap - rows
    local = qkv_weight.shape[2]
    hidden = mlp_in.shape[1]
    share = qkv_weight.shape[0]
    pairs = local // PAIR
    per_call = min(PAIRS_PER_CALL, pairs)
    calls = pairs // per_call
    me = lax.axis_index("ctx")
    shard_at = (lax.axis_index("dp") * n_ctx + me) * share

    small = jnp.concatenate([norm_gain, norm_bias, out_bias], axis=0)
    small = jnp.pad(small.T, ((0, 0), (0, PAIR - small.shape[0])))
    w_kv = jnp.stack(
        [qkv_weight[:, 1].reshape(share, pairs, PAIR), qkv_weight[:, 2].reshape(share, pairs, PAIR)],
        axis=2,
    ).reshape(share, 2 * local)
    first = gather_rows(jnp.concatenate([w_kv, small], axis=1))
    w_kv = first[:, : 2 * local]
    small = first[:, 2 * local : 2 * local + 6].T.astype(F32)
    gains, shifts, biases = small[0:2], small[2:4], small[4:6]
    second = gather_rows(jnp.concatenate([qkv_weight[:, 0], out_weight.T], axis=1))
    w_q, w_out = second[:, :local], second[:, local:]
    w_in = lax.all_gather(mlp_in, ("dp", "ctx"), axis=0, tiled=True)
    w_down = lax.all_gather(mlp_out.T, ("dp", "ctx"), axis=0, tiled=True)

    over = jnp.maximum(lengths - rows, 0)
    lack = jnp.maximum(rows - lengths, 0)
    over_at = jnp.cumsum(over) - over
    lack_at = jnp.cumsum(lack) - lack
    my_length = lengths[me]
    row = lax.iota(jnp.int32, rows)
    own = row < my_length
    need = jnp.where(own, -1, lack_at[me] + row - my_length)
    column = lax.iota(jnp.int32, n_ctx * spare)
    owner = (column // spare) ^ me
    source = jnp.where(column % spare < over[owner], over_at[owner] + column % spare, -2)
    pick = (need[:, None] == source[None, :]).astype(BF)

    def take(v):
        blocks = jnp.concatenate(gather_ctx(v[rows:]), axis=0)
        return jnp.where(own[:, None], v[:rows], dot_nn(pick, blocks).astype(BF))

    def give(v):
        blocks = dot_tn(pick, v).astype(BF)
        near, far = blocks[spare : 2 * spare], blocks[3 * spare :]
        got = swap_core(jnp.concatenate([near, far], axis=0))
        back = swap_y(blocks[2 * spare : 3 * spare] + got[spare:])
        kept = jnp.where(own[:, None], v, jnp.zeros_like(v))
        return jnp.concatenate([kept, got[:spare] + back], axis=0)[None]

    x = take(tokens[0]).astype(F32)
    d_down = take(cotangent[0])

    unit_one, rstd_one = norm_parts(x)
    h1 = (unit_one * gains[0] + shifts[0]).astype(BF)
    kv_bias = jnp.stack(
        [jnp.zeros((pairs, PAIR), F32), qv_bias[1].reshape(pairs, PAIR)], axis=1
    ).reshape(2 * local)
    kv_blocks = []
    for call in range(calls):
        at = slice(call * per_call * 2 * PAIR, (call + 1) * per_call * 2 * PAIR)
        kv = (dot_nn(h1, w_kv[:, at]) + kv_bias[at]).astype(BF)
        kv_blocks.append(gather_ctx(kv))
    query = (dot_nn(h1, w_q) + qv_bias[0]).astype(BF)
    attn, lse = [], []
    for call in range(calls):
        o, l = attend(query, kv_blocks[call], call)
        attn.append(o)
        lse.append(l)
    attended = jnp.concatenate([o.astype(BF) for o in attn], axis=1)
    x_one = x + (sum_tp(dot_nt(attended, w_out).astype(BF)) + biases[0])
    unit_two, rstd_two = norm_parts(x_one)
    h2 = (unit_two * gains[1] + shifts[1]).astype(BF)
    act, d_pre, y_part, back_part, mlp_bias_grad = mlp(h2, d_down, w_in, w_down, mlp_bias[None])
    d_h2 = sum_tp(back_part)
    grad_in = lax.psum_scatter(
        dot_tn(h2, d_pre).astype(BF), ("dp", "ctx"), scatter_dimension=0, tiled=True
    ).astype(F32)
    grad_down = (
        lax.psum_scatter(
            dot_tn(d_down, act).astype(BF), ("dp", "ctx"), scatter_dimension=0, tiled=True
        )
        .astype(F32)
        .T
    )

    d_x_one = d_down.astype(F32) + norm_back(d_h2, unit_two, rstd_two, gains[1])
    d_branch = d_x_one.astype(BF)
    d_att = dot_nn(d_branch, w_out).astype(BF)
    result = give((x_one + (sum_tp(y_part) + biases[1])).astype(BF))

    d_query, d_kv = [], []
    for call in range(calls):
        dq, keep, send = attend_back(query, d_att, attn[call], lse[call], kv_blocks[call], call)
        got = swap_core(send)
        far = swap_y((keep[rows:].astype(F32) + got[rows:].astype(F32)).astype(BF))
        d_kv.append(
            (keep[:rows].astype(F32) + got[:rows].astype(F32) + far.astype(F32)).astype(BF)
        )
        d_query.append(dq)
    d_query = jnp.concatenate(d_query, axis=1)
    d_kv = jnp.concatenate(d_kv, axis=1)

    attn_back = dot_nt(d_query, w_q) + dot_nt(d_kv, w_kv)
    attn_back = attn_back.astype(BF)
    d_h1 = sum_tp(attn_back)
    grad_tokens = give((d_x_one + norm_back(d_h1, unit_one, rstd_one, gains[0])).astype(BF))

    grad_attn = jnp.concatenate(
        [dot_tn(h1, d_query), dot_tn(h1, d_kv), dot_tn(d_branch, attended)], axis=1
    ).astype(BF)
    grad_attn = scatter_rows(grad_attn)
    grad_q = grad_attn[:, :local]
    grad_kv = grad_attn[:, local : 3 * local].reshape(share, pairs, 2, PAIR)
    grad_qkv = jnp.stack(
        [grad_q, grad_kv[:, :, 0].reshape(share, local), grad_kv[:, :, 1].reshape(share, local)],
        axis=1,
    )
    grad_out = grad_attn[:, 3 * local :].T

    q_sum = jnp.sum(d_query.astype(F32), axis=0)
    v_sum = jnp.sum(d_kv.astype(F32), axis=0).reshape(pairs, 2, PAIR)[:, 1].reshape(local)
    sums = jnp.concatenate([
        jnp.sum(d_h1 * unit_one, axis=0),
        jnp.sum(d_h2 * unit_two, axis=0),
        jnp.sum(d_h1, axis=0),
        jnp.sum(d_h2, axis=0),
        jnp.sum(d_branch.astype(F32), axis=0),
        jnp.sum(d_down.astype(F32), axis=0),
        q_sum,
        v_sum,
        mlp_bias_grad[0],
    ])
    sums = sum_small(sums.reshape(-1, PAIR)).reshape(-1)
    wide = lax.dynamic_slice(sums[: 6 * width].reshape(6, width), (0, shard_at), (6, share))
    qv_grad = sums[6 * width : 6 * width + 2 * local].reshape(2, local)
    mlp_bias_sum = sums[6 * width + 2 * local :]
    return (
        result,
        grad_tokens,
        wide[0:2],
        wide[2:4],
        grad_qkv,
        qv_grad,
        grad_out,
        grad_in,
        mlp_bias_sum,
        grad_down,
        wide[4:6],
    )


def solution(mesh):
    in_specs = (
        P("dp", "ctx", None),
        P(),
        P(None, ("dp", "ctx")),
        P(None, ("dp", "ctx")),
        P(("dp", "ctx"), None, "tp"),
        P(None, "tp"),
        P("tp", ("dp", "ctx")),
        P(("dp", "ctx"), "tp"),
        P("tp"),
        P("tp", ("dp", "ctx")),
        P(None, ("dp", "ctx")),
        P("dp", "ctx", None),
    )
    out_specs = (
        P("dp", "ctx", None),
        P("dp", "ctx", None),
        P(None, ("dp", "ctx")),
        P(None, ("dp", "ctx")),
        P(("dp", "ctx"), None, "tp"),
        P(None, "tp"),
        P("tp", ("dp", "ctx")),
        P(("dp", "ctx"), "tp"),
        P("tp"),
        P("tp", ("dp", "ctx")),
        P(None, ("dp", "ctx")),
    )
    return jax.shard_map(body, mesh=mesh, in_specs=in_specs, out_specs=out_specs, check_vma=False)
```

```python
import functools
import math

import jax
import jax.numpy as jnp
from jax import lax
from jax.experimental import pallas as pl
from jax.experimental.pallas import tpu as pltpu
from jax.sharding import PartitionSpec as P

HD = 64
PAIR = 2 * HD
EPS = 1e-06
LOG2E = 1.4426950408889634
BF = jnp.bfloat16
F32 = jnp.float32
VMEM_LIMIT = 56 * 1024 * 1024
PAIRS_PER_CALL = 1
PARTS = 2
KEY_TILE = 512
QUERY_TILE = 256
HIDDEN_TILE = 256
WEIGHT = 4


def dot_nt(a, b):
    return lax.dot_general(a, b, (((1,), (1,)), ((), ())), preferred_element_type=F32)


def dot_tn(a, b):
    return lax.dot_general(a, b, (((0,), (0,)), ((), ())), preferred_element_type=F32)


def dot_nn(a, b):
    return jnp.dot(a, b, preferred_element_type=F32)


def swap_core(v):
    return lax.ppermute(v, "ctx", [(0, 1), (1, 0), (2, 3), (3, 2)])


def swap_y(v):
    return lax.ppermute(v, "ctx", [(0, 2), (2, 0), (1, 3), (3, 1)])


def after(v, *earlier):
    if not earlier:
        return v
    whole = pl.BlockSpec(memory_space=pl.ANY)
    return pl.pallas_call(
        lambda *refs: None,
        in_specs=[whole] * (1 + len(earlier)),
        out_specs=whole,
        out_shape=jax.ShapeDtypeStruct(v.shape, v.dtype),
        input_output_aliases={0: 0},
        name="after",
    )(v, *earlier)


def gather_ctx(v, over, *earlier):
    return v, over, swap_core(after(v, *earlier)), swap_core(after(over, *earlier))


def sum_tp(part, *earlier):
    if lax.axis_size("tp") == 2:
        other = after(lax.ppermute(part, "tp", [(0, 1), (1, 0)]), *earlier)
        return part.astype(F32) + other.astype(F32)
    return after(lax.psum(part, "tp"), *earlier).astype(F32)


def swap_line(v, bit):
    return lax.ppermute(v, "dp", [(i, i ^ bit) for i in range(lax.axis_size("dp"))])


def line_bits():
    return [1 << k for k in reversed(range(lax.axis_size("dp").bit_length() - 1))]


def gather_line(v, *earlier):
    z = lax.axis_index("dp")
    v = v[None]
    for stage, bit in enumerate(line_bits()):
        if stage:
            v = after(v, *earlier)
        other = swap_line(v, bit)
        odd = (z & bit) != 0
        pair = jnp.stack([jnp.where(odd, other, v), jnp.where(odd, v, other)], axis=1)
        v = pair.reshape(-1, *v.shape[1:])
    return v


def gather_rest(v, over, *earlier):
    me = lax.axis_index("ctx")
    odd_core, odd_y = (me & 1) == 1, (me >> 1) == 1
    b0, b2, b1, b3 = gather_ctx(v, over, *earlier)
    lo, hi = jnp.where(odd_core, b1, b0), jnp.where(odd_core, b0, b1)
    lo_far, hi_far = jnp.where(odd_core, b3, b2), jnp.where(odd_core, b2, b3)
    whole = jnp.stack(
        [
            jnp.where(odd_y, lo_far, lo),
            jnp.where(odd_y, hi_far, hi),
            jnp.where(odd_y, lo, lo_far),
            jnp.where(odd_y, hi, hi_far),
        ],
        axis=1,
    )
    return whole.reshape(-1, v.shape[2])


def scatter_stages(v, waits):
    n = lax.axis_size("dp")
    me = lax.axis_index("ctx")
    z = lax.axis_index("dp")
    rows, columns = v.shape
    v = v.reshape(n, 2, 2, rows // (4 * n), columns)

    waits = iter(waits)

    def halve(a, i, axis, swap):
        keep = lax.dynamic_index_in_dim(a, i, axis, keepdims=False)
        send = lax.dynamic_index_in_dim(a, 1 - i, axis, keepdims=False)
        other = after(swap(send), *next(waits, []))
        return keep.astype(F32) + other.astype(F32)

    v = halve(v, me & 1, 2, swap_core).astype(BF)
    yield v
    v = halve(v, me >> 1, 1, swap_y)
    bit = 1
    while bit < n:
        v = v.astype(BF)
        yield v
        v = v.reshape(v.shape[0] // 2, 2, *v.shape[1:])
        v = halve(v, (z // bit) & 1, 1, functools.partial(swap_line, bit=bit))
        bit *= 2
    yield v[0]


def sum_stages(v):
    v = v + swap_core(v)
    yield v
    v = v + swap_y(v)
    yield v
    for bit in line_bits():
        v = v + swap_line(v, bit)
        yield v


def attend_kernel(scale, q_ref, k0, k1, k2, k3, *refs):
    o_ref, low_ref, lse_ref = refs[-3:]
    rows = q_ref.shape[0]
    tile = min(QUERY_TILE, rows)
    first = lax.broadcasted_iota(jnp.int32, (1, PAIR), 1) < HD

    def step(i, carry):
        at = pl.ds(pl.multiple_of(i * tile, tile), tile)
        q = q_ref[at, :]
        outs = []
        for h in range(2):
            mine = first if h == 0 else jnp.logical_not(first)
            q_h = jnp.where(mine, q, jnp.zeros_like(q))
            scores = [dot_nt(q_h, k[:, :PAIR]) for k in (k0, k1, k2, k3)]
            top = functools.reduce(
                jnp.maximum, [jnp.max(s, axis=1, keepdims=True) for s in scores]
            )
            acc = None
            for s, k in zip(scores, (k0, k1, k2, k3)):
                p = jnp.exp2((s - top) * scale).astype(BF)
                v = k[:, PAIR:]
                term = dot_nn(p, jnp.where(mine, v, jnp.ones_like(v)))
                acc = term if acc is None else acc + term
            total = pltpu.roll(acc, HD, 1)
            outs.append(acc / total)
            lse = jnp.transpose(top * scale + jnp.log2(total))
            lse_ref[0, pl.ds(h, 1), at] = lse[h * HD : h * HD + 1, :]
        out = jnp.where(first, outs[0], outs[1])
        o_ref[at, :] = out
        low_ref[at, :] = out.astype(BF)
        return carry

    lax.fori_loop(0, rows // tile, step, 0)


def key_specs(rows):
    return [pl.BlockSpec((rows, 2 * PAIR), lambda i: (0, i))] * 4


def attend(q, blocks, call, calls, held, *earlier):
    rows, all_width = q.shape
    width = all_width // calls
    pairs = width // PAIR
    base = call * pairs
    keys = 4 * rows
    spec = pl.BlockSpec((rows, PAIR), lambda i: (0, base + i))
    return pl.pallas_call(
        functools.partial(attend_kernel, LOG2E / math.sqrt(HD)),
        grid=(pairs,),
        in_specs=[spec]
        + key_specs(rows)
        + [pl.BlockSpec(memory_space=pl.ANY)] * (len(held) + len(earlier)),
        out_specs=[spec, spec, pl.BlockSpec((1, 8, rows), lambda i: (base + i, 0, 0))],
        out_shape=[
            jax.ShapeDtypeStruct((rows, all_width), F32),
            jax.ShapeDtypeStruct((rows, all_width), BF),
            jax.ShapeDtypeStruct((calls * pairs, 8, rows), F32),
        ],
        input_output_aliases={5 + i: i for i in range(len(held))},
        cost_estimate=pl.CostEstimate(
            flops=(16 * rows * keys * width) // WEIGHT,
            bytes_accessed=(rows * width * 16) // WEIGHT,
            transcendentals=(rows * keys * width // HD) // WEIGHT,
        ),
        compiler_params=pltpu.CompilerParams(vmem_limit_bytes=VMEM_LIMIT),
        name="attend",
    )(q, *blocks, *held, *earlier)


def attend_back_kernel(scale, factor, blocks, last, q_ref, d_ref, o_ref, lse_ref, *refs):
    rows = q_ref.shape[0]
    keys = 2 * rows
    tile = min(KEY_TILE, rows)
    kv = refs[-2]
    dq_turned = refs[-1]
    dq_ref, out_ref = refs[-4:-2]
    start = 0
    for block in refs[:blocks]:
        kv[start : start + block.shape[0], :] = block[...]
        start += block.shape[0]
    first = lax.broadcasted_iota(jnp.int32, (1, PAIR), 1) < HD
    d = d_ref[...]
    q = q_ref[...]
    prod = jnp.transpose(d.astype(F32) * o_ref[...])
    halves = []
    for h in range(2):
        mine = first if h == 0 else jnp.logical_not(first)
        halves.append((
            jnp.where(mine, q, jnp.zeros_like(q)),
            jnp.where(mine, d, jnp.zeros_like(d)),
            lse_ref[0, h : h + 1, :],
            jnp.sum(prod[h * HD : (h + 1) * HD, :], axis=0, keepdims=True),
        ))
    dq_turned[...] = refs[blocks][...] if last else jnp.zeros_like(dq_turned)

    def step(i, carry):
        at = pl.ds(pl.multiple_of(i * tile, tile), tile)
        k = kv[at, :PAIR]
        v = kv[at, PAIR:]
        k_turned = jnp.transpose(k)
        dk = dv = None
        for h, (q_h, d_h, lse, delta) in enumerate(halves):
            prob = jnp.exp2(dot_nt(k, q_h) * scale - lse)
            d_score = (prob * (dot_nt(v, d_h) - delta)).astype(BF)
            dv_h = dot_nn(prob.astype(BF), d_h)
            dk_h = dot_nn(d_score, q_h)
            dv = dv_h if dv is None else dv + dv_h
            dk = dk_h if dk is None else dk + dk_h
            part = slice(h * HD, (h + 1) * HD)
            dq_turned[part, :] += dot_nn(k_turned[part, :], d_score)
        out_ref[at, :PAIR] = (dk * factor).astype(BF)
        out_ref[at, PAIR:] = dv.astype(BF)
        return carry

    lax.fori_loop(0, keys // tile, step, 0)
    if last:
        dq_ref[...] = (jnp.transpose(dq_turned[...]) * factor).astype(BF)
    else:
        dq_ref[...] = dq_turned[...]


def attend_back(q, d_att, o, lse, blocks, call, partial, *earlier):
    rows = q.shape[0]
    width = blocks[0].shape[1] // 2
    pairs = width // PAIR
    base = call * pairs
    keys = 2 * rows
    last = partial is not None
    wide = pl.BlockSpec((rows, PAIR), lambda i: (0, base + i))
    narrow = pl.BlockSpec((rows, PAIR), lambda i: (0, i))
    turned = pl.BlockSpec((PAIR, rows), lambda i: (i, 0))
    held = [partial] if last else []
    return pl.pallas_call(
        functools.partial(
            attend_back_kernel, LOG2E / math.sqrt(HD), 1.0 / math.sqrt(HD), len(blocks), last
        ),
        grid=(pairs,),
        in_specs=[wide, wide, wide, pl.BlockSpec((1, 8, rows), lambda i: (base + i, 0, 0))]
        + [pl.BlockSpec((b.shape[0], 2 * PAIR), lambda i: (0, i)) for b in blocks]
        + [turned] * len(held)
        + [pl.BlockSpec(memory_space=pl.ANY)] * len(earlier),
        out_specs=[
            narrow if last else turned,
            pl.BlockSpec((keys, 2 * PAIR), lambda i: (0, i)),
        ],
        out_shape=[
            jax.ShapeDtypeStruct((rows, width), BF)
            if last
            else jax.ShapeDtypeStruct((width, rows), F32),
            jax.ShapeDtypeStruct((keys, 2 * width), BF),
        ],
        scratch_shapes=[
            pltpu.VMEM((keys, 2 * PAIR), BF),
            pltpu.VMEM((PAIR, rows), F32),
        ],
        cost_estimate=pl.CostEstimate(
            flops=(40 * rows * keys * width) // WEIGHT,
            bytes_accessed=(rows * width * 40) // WEIGHT,
            transcendentals=(rows * keys * width // HD) // WEIGHT,
        ),
        compiler_params=pltpu.CompilerParams(vmem_limit_bytes=VMEM_LIMIT),
        name="attend_back",
    )(q, d_att, o, lse, *blocks, *held, *earlier)


def mlp_kernel(h2_ref, d_ref, in_ref, down_ref, bias_ref, *refs):
    pair_ref, y_ref, back_ref, bias_grad_ref, y_acc, back_acc = refs[-6:]
    i = pl.program_id(0)
    w_in, w_down = in_ref[...], down_ref[...]
    pre = dot_nn(h2_ref[...], w_in) + bias_ref[...]
    d_act = dot_nn(d_ref[...], w_down)
    below = 0.5 * (1.0 + lax.erf(pre * math.sqrt(0.5)))
    act = (pre * below).astype(BF)
    slope = below + pre * (jnp.exp(-0.5 * pre * pre) * (1.0 / math.sqrt(2.0 * math.pi)))
    d_pre = (d_act * slope).astype(BF)
    pair_ref[0] = d_pre
    pair_ref[1] = act
    bias_grad_ref[...] = jnp.sum(d_pre.astype(F32), axis=0, keepdims=True)
    y = dot_nt(act, w_down)
    back = dot_nt(d_pre, w_in)

    @pl.when(i == 0)
    def _():
        y_acc[...] = y
        back_acc[...] = back

    @pl.when(i > 0)
    def _():
        y_acc[...] += y
        back_acc[...] += back

    @pl.when(i == pl.num_programs(0) - 1)
    def _():
        y_ref[...] = y_acc[...].astype(BF)
        back_ref[...] = back_acc[...].astype(BF)


def mlp(h2, d_down, weights, bias, held, part, parts):
    rows, width = h2.shape
    hidden = bias.shape[1]
    tile = min(HIDDEN_TILE, hidden)
    tiles = hidden // tile
    whole = pl.BlockSpec((rows, width), lambda i: (0, 0))
    mine = pl.BlockSpec((rows, width), lambda i: (part, 0))
    w_in = pl.BlockSpec((width, tile), lambda i: (0, i))
    w_down = pl.BlockSpec((width, tile), lambda i: (0, tiles + i))
    line = pl.BlockSpec((1, tile), lambda i: (0, i))
    more = () if held is None else (held,)
    return pl.pallas_call(
        mlp_kernel,
        grid=(tiles,),
        in_specs=[whole, mine, w_in, w_down, line]
        + [pl.BlockSpec(memory_space=pl.ANY)] * len(more),
        out_specs=[pl.BlockSpec((2, rows, tile), lambda i: (0, part, i)), whole, whole, line],
        out_shape=[
            jax.ShapeDtypeStruct((2, rows * parts, hidden), BF),
            jax.ShapeDtypeStruct((rows, width), BF),
            jax.ShapeDtypeStruct((rows, width), BF),
            jax.ShapeDtypeStruct((1, hidden), F32),
        ],
        scratch_shapes=[pltpu.VMEM((rows, width), F32), pltpu.VMEM((rows, width), F32)],
        input_output_aliases={5: 0} if more else {},
        cost_estimate=pl.CostEstimate(
            flops=(8 * rows * width * hidden) // WEIGHT,
            bytes_accessed=(4 * width * hidden + 4 * rows * hidden + 8 * rows * width) // WEIGHT,
            transcendentals=(rows * hidden) // WEIGHT,
        ),
        compiler_params=pltpu.CompilerParams(vmem_limit_bytes=VMEM_LIMIT),
        name="mlp",
    )(h2, d_down, weights, weights, bias, *more)


def norm_parts(v):
    mean = jnp.mean(v, axis=-1, keepdims=True)
    centred = v - mean
    var = jnp.mean(centred * centred, axis=-1, keepdims=True)
    rstd = lax.rsqrt(var + EPS)
    return centred * rstd, rstd


def norm_back(d, unit, rstd, gain):
    d_unit = d * gain
    return rstd * (
        d_unit
        - jnp.mean(d_unit, axis=-1, keepdims=True)
        - unit * jnp.mean(d_unit * unit, axis=-1, keepdims=True)
    )


def body(
    tokens,
    lengths,
    norm_gain,
    norm_bias,
    qkv_weight,
    qv_bias,
    out_weight,
    mlp_in,
    mlp_bias,
    mlp_out,
    out_bias,
    cotangent,
):
    _, cap, width = tokens.shape
    n_ctx = lax.axis_size("ctx")
    slots = n_ctx * cap
    rows = 3 * slots // 4 // n_ctx
    spare = cap - rows
    local = qkv_weight.shape[2]
    hidden = mlp_in.shape[1]
    share = qkv_weight.shape[0]
    pairs = local // PAIR
    per_call = min(PAIRS_PER_CALL, pairs)
    calls = pairs // per_call
    me = lax.axis_index("ctx")

    small = jnp.concatenate([norm_gain, norm_bias, out_bias], axis=0)
    small = jnp.pad(small.T, ((0, 0), (0, PAIR - small.shape[0])))
    w_kv = jnp.stack(
        [qkv_weight[:, 1].reshape(share, pairs, PAIR), qkv_weight[:, 2].reshape(share, pairs, PAIR)],
        axis=2,
    ).reshape(share, 2 * local)
    tokens_far = swap_y(tokens[0, rows:])
    line = gather_line(jnp.concatenate([qkv_weight[:, 0], w_kv, small], axis=1), tokens_far)
    over = jnp.maximum(lengths - rows, 0)
    lack = jnp.maximum(rows - lengths, 0)
    row = lax.iota(jnp.int32, rows)
    column = lax.iota(jnp.int32, n_ctx * spare)
    owner = (column // spare) ^ me
    slot = column % spare
    my_length = jnp.int32(0)
    my_lack_at = jnp.int32(0)
    source = jnp.full((n_ctx * spare,), -2, jnp.int32)
    over_at = lack_at = jnp.int32(0)
    for c in range(n_ctx):
        my_length = jnp.where(me == c, lengths[c], my_length)
        my_lack_at = jnp.where(me == c, lack_at, my_lack_at)
        source = jnp.where((owner == c) & (slot < over[c]), over_at + slot, source)
        over_at, lack_at = over_at + over[c], lack_at + lack[c]
    own = row < my_length
    need = jnp.where(own, -1, my_lack_at + row - my_length)
    source = source.reshape(n_ctx, spare)
    source = jnp.concatenate([source[0], source[2], source[1], source[3]])
    pick = (need[:, None] == source[None, :]).astype(BF)

    def take(v, over):
        blocks = jnp.concatenate(gather_ctx(v[rows:], over), axis=0)
        return jnp.where(own[:, None], v[:rows], dot_nn(pick, blocks).astype(BF))

    def give_near(v):
        blocks = dot_tn(pick[:, spare:], v).astype(BF)
        return v, blocks, swap_core(blocks[spare:])

    def give_far(v, blocks, got):
        back = swap_y(blocks[:spare] + got[spare:])
        kept = jnp.where(own[:, None], v, jnp.zeros_like(v))
        return jnp.concatenate([kept, got[:spare] + back], axis=0)[None], back

    x_low = take(tokens[0], tokens_far)
    x = x_low.astype(F32)
    unit_one, rstd_one = norm_parts(x)

    line = after(line, x_low)
    line_far = swap_y(line)
    rest = jnp.concatenate([mlp_in, mlp_out.T, out_weight.T], axis=1)
    rest = lax.all_gather(after(rest, line_far), ("dp", "ctx"), axis=0, tiled=True)
    w_out = rest[:, 2 * hidden :]
    first = gather_rest(line, line_far)
    w_q, w_kv, w_qkv = first[:, :local], first[:, local : 3 * local], first[:, : 3 * local]
    small = first[:, 3 * local : 3 * local + 6].T.astype(F32)
    gains, shifts, biases = small[0:2], small[2:4], small[4:6]
    h1 = (unit_one * gains[0] + shifts[0]).astype(BF)
    kv_bias = jnp.stack(
        [jnp.zeros((pairs, PAIR), F32), qv_bias[1].reshape(pairs, PAIR)], axis=1
    ).reshape(2 * local)
    query = (dot_nn(h1, w_q) + qv_bias[0]).astype(BF)
    kvs, far = [], []
    for call in range(calls):
        at = slice(call * per_call * 2 * PAIR, (call + 1) * per_call * 2 * PAIR)
        kvs.append((dot_nn(h1, w_kv[:, at]) + kv_bias[at]).astype(BF))
    held, far, kv_blocks = (), [], []
    for call in range(min(2, calls)):
        kvs[call] = after(kvs[call], *far)
        far.append(swap_y(kvs[call]))
    for call in range(calls):
        kv_blocks.append(gather_ctx(kvs[call], after(far[call], *held[2:])))
        held = attend(query, kv_blocks[call], call, calls, held)
        if call + 2 < calls:
            kvs[call + 2] = after(kvs[call + 2], held[2])
            far.append(swap_y(kvs[call + 2]))
    attn, attended, lse = held
    cot_far = swap_y(after(cotangent[0, rows:], far[-1]))
    d_down = take(cotangent[0], after(cot_far, lse))
    parts = PARTS
    mine = rows // parts
    pair = None
    x_one, y_parts, back_parts, h2, mlp_bias_grad = [], [], [], [], 0.0
    for part in range(parts):
        at = slice(part * mine, (part + 1) * mine)
        branch = sum_tp(dot_nt(attended[at], w_out).astype(BF), *y_parts)
        x_part = x[at] + (branch + biases[0])
        unit, rstd = norm_parts(x_part)
        h2_part = (unit * gains[1] + shifts[1]).astype(BF)
        pair, y_part, back_part, bias_part = mlp(
            h2_part, d_down, rest, mlp_bias[None], pair, part, parts
        )
        x_one.append(x_part)
        h2.append(h2_part)
        y_parts.append(y_part)
        back_parts.append(back_part)
        mlp_bias_grad = mlp_bias_grad + bias_part
    d_h2 = [sum_tp(v, y_parts[-1]) for v in back_parts[:-1]]
    sides = after(jnp.stack([jnp.concatenate(h2, axis=0), d_down]), *d_h2)
    grads = jnp.einsum("btd,btf->bdf", sides, pair, preferred_element_type=F32).astype(BF)
    d_h2.append(sum_tp(back_parts[-1], grads))
    grad_mlp = lax.psum_scatter(grads, ("dp", "ctx"), scatter_dimension=1, tiled=True)
    grad_in = grad_mlp[0].astype(F32)
    grad_down = grad_mlp[1].astype(F32).T

    d_x_one, d_att, gain_two, shift_two = [], [], 0.0, 0.0
    for part in range(parts):
        at = slice(part * mine, (part + 1) * mine)
        unit, rstd = norm_parts(x_one[part])
        d_part = d_down[at].astype(F32) + norm_back(d_h2[part], unit, rstd, gains[1])
        d_x_one.append(d_part)
        d_att.append(dot_nn(d_part.astype(BF), w_out).astype(BF))
        gain_two = gain_two + jnp.sum(d_h2[part] * unit, axis=0)
        shift_two = shift_two + jnp.sum(d_h2[part], axis=0)
    d_x_one = jnp.concatenate(d_x_one, axis=0)
    d_att = jnp.concatenate(d_att, axis=0)
    d_branch = d_x_one.astype(BF)
    grad_out = dot_tn(d_branch, attended).astype(BF)
    sums = [
        gain_two,
        shift_two,
        jnp.sum(d_branch.astype(F32), axis=0),
        jnp.sum(d_down.astype(F32), axis=0),
    ]

    d_query, d_kv = [], []
    earlier = [grads]
    result_back = []
    for call in range(calls):
        near, over, *side = kv_blocks[call]
        partial, send = attend_back(query, d_att, attn, lse, side, call, None, *earlier)
        got = swap_core(send)
        dq, keep = attend_back(query, d_att, attn, lse, (near, over), call, partial)
        if call == calls - 1 and call > 2:
            got = after(got, result_back)
        got = after(got, keep)
        if call == min(1, calls - 1):
            result = give_near(
                jnp.concatenate([
                    (x_part + (sum_tp(after(y_part, d_att), keep) + biases[1])).astype(BF)
                    for x_part, y_part in zip(x_one, y_parts)
                ])
            )
        if call == min(2, calls - 1):
            result, result_back = give_far(*result[:2], after(result[2], keep))
        mid = (keep[rows:].astype(F32) + got[rows:].astype(F32)).astype(BF)
        far_kv = swap_y(mid)
        d_kv.append((keep[:rows], got[:rows], far_kv))
        d_query.append(dq)
        earlier = [mid]
        if call == min(1, calls - 1):
            earlier.append(result[2])
        if call == min(2, calls - 1):
            earlier.append(grad_mlp)
    d_kv = [
        (a.astype(F32) + b.astype(F32) + c.astype(F32)).astype(BF) for a, b, c in d_kv
    ]
    d_qkv = jnp.concatenate(d_query + d_kv, axis=1)
    qkv_sum = jnp.sum(d_qkv.astype(F32), axis=0)
    v_sum = qkv_sum[local:].reshape(pairs, 2, PAIR)[:, 1].reshape(local)
    few = sum_stages(
        jnp.concatenate([qkv_sum[:local], v_sum, mlp_bias_grad[0]]).reshape(-1, PAIR)
    )
    attn_back = dot_nt(d_qkv, w_qkv)
    sums = [jnp.sum(attn_back * unit_one, axis=0), jnp.sum(attn_back, axis=0), *sums]
    sums = jnp.pad(jnp.stack(sums), ((0, PAIR - len(sums)), (0, 0))).T
    grad_attn = jnp.concatenate(
        [dot_tn(h1, d_qkv).astype(BF), grad_out, sums.astype(BF)], axis=1
    )
    attn_low = attn_back.astype(BF)
    waits = [[], [], [], []]
    scatter = scatter_stages(grad_attn, waits)
    next(scatter)
    d_h1 = sum_tp(attn_low, next(scatter))
    grad_rows = (d_x_one + norm_back(d_h1, unit_one, rstd_one, gains[0])).astype(BF)
    rows_back, blocks, got = give_near(grad_rows)
    grad_tokens, tokens_back = give_far(rows_back, blocks, got)
    waits[3].append(tokens_back)
    waits[2].append(grad_rows)
    for few_sums in few:
        pass
    few_sums = few_sums.reshape(-1)
    for grad_attn in scatter:
        pass
    grad_qkv = grad_attn[:, : 3 * local]
    grad_out = grad_attn[:, 3 * local : 4 * local].T
    sums = grad_attn[:, 4 * local : 4 * local + 6].T
    ones = sums[:2]
    if lax.axis_size("tp") == 2:
        ones = ones + lax.ppermute(ones, "tp", [(0, 1), (1, 0)])
    else:
        ones = lax.psum(ones, "tp")
    grad_kv = grad_qkv[:, local:].reshape(share, pairs, 2, PAIR)
    grad_qkv = jnp.stack(
        [
            grad_qkv[:, :local],
            grad_kv[:, :, 0].reshape(share, local),
            grad_kv[:, :, 1].reshape(share, local),
        ],
        axis=1,
    )

    grad_gain = jnp.stack([ones[0], sums[2]])
    grad_shift = jnp.stack([ones[1], sums[3]])
    grad_out_bias = sums[4:6]
    qv_grad = few_sums[: 2 * local].reshape(2, local)
    mlp_bias_sum = few_sums[2 * local :]
    return (
        result,
        grad_tokens,
        grad_gain,
        grad_shift,
        grad_qkv,
        qv_grad,
        grad_out,
        grad_in,
        mlp_bias_sum,
        grad_down,
        grad_out_bias,
    )


def solution(mesh):
    in_specs = (
        P("dp", "ctx", None),
        P(),
        P(None, ("dp", "ctx")),
        P(None, ("dp", "ctx")),
        P(("dp", "ctx"), None, "tp"),
        P(None, "tp"),
        P("tp", ("dp", "ctx")),
        P(("dp", "ctx"), "tp"),
        P("tp"),
        P("tp", ("dp", "ctx")),
        P(None, ("dp", "ctx")),
        P("dp", "ctx", None),
    )
    out_specs = (
        P("dp", "ctx", None),
        P("dp", "ctx", None),
        P(None, ("dp", "ctx")),
        P(None, ("dp", "ctx")),
        P(("dp", "ctx"), None, "tp"),
        P(None, "tp"),
        P("tp", ("dp", "ctx")),
        P(("dp", "ctx"), "tp"),
        P("tp"),
        P("tp", ("dp", "ctx")),
        P(None, ("dp", "ctx")),
    )
    return jax.shard_map(body, mesh=mesh, in_specs=in_specs, out_specs=out_specs, check_vma=False)
```

```python
import functools
import math

import jax
import jax.numpy as jnp
from jax import lax
from jax.experimental import pallas as pl
from jax.experimental.pallas import tpu as pltpu
from jax.sharding import PartitionSpec as P

HD = 64
PAIR = 2 * HD
EPS = 1e-06
LOG2E = 1.4426950408889634
BF = jnp.bfloat16
F32 = jnp.float32
VMEM_LIMIT = 56 * 1024 * 1024
PAIRS_PER_CALL = 1
PARTS = 2
KEY_TILE = 768
QUERY_TILE = 256
HIDDEN_TILE = 1024
WEIGHT = 4


def dot_nt(a, b):
    return lax.dot_general(a, b, (((1,), (1,)), ((), ())), preferred_element_type=F32)


def dot_tn(a, b):
    return lax.dot_general(a, b, (((0,), (0,)), ((), ())), preferred_element_type=F32)


def dot_nn(a, b):
    return jnp.dot(a, b, preferred_element_type=F32)


def swap_core(v):
    return lax.ppermute(v, "ctx", [(0, 1), (1, 0), (2, 3), (3, 2)])


def swap_y(v):
    return lax.ppermute(v, "ctx", [(0, 2), (2, 0), (1, 3), (3, 1)])


def after(v, *earlier):
    if not earlier:
        return v
    whole = pl.BlockSpec(memory_space=pl.ANY)
    return pl.pallas_call(
        lambda *refs: None,
        in_specs=[whole] * (1 + len(earlier)),
        out_specs=whole,
        out_shape=jax.ShapeDtypeStruct(v.shape, v.dtype),
        input_output_aliases={0: 0},
        name="after",
    )(v, *earlier)


def gather_ctx(v, over, *earlier):
    return v, over, swap_core(after(v, *earlier)), swap_core(after(over, *earlier))


def sum_tp(part, *earlier):
    if lax.axis_size("tp") == 2:
        other = after(lax.ppermute(part, "tp", [(0, 1), (1, 0)]), *earlier)
        return part.astype(F32) + other.astype(F32)
    return after(lax.psum(part, "tp"), *earlier).astype(F32)


def swap_line(v, bit):
    return lax.ppermute(v, "dp", [(i, i ^ bit) for i in range(lax.axis_size("dp"))])


def line_bits():
    return [1 << k for k in reversed(range(lax.axis_size("dp").bit_length() - 1))]


def gather_line(v, *earlier):
    z = lax.axis_index("dp")
    v = v[None]
    for stage, bit in enumerate(line_bits()):
        if stage:
            v = after(v, *earlier)
        other = swap_line(v, bit)
        odd = (z & bit) != 0
        pair = jnp.stack([jnp.where(odd, other, v), jnp.where(odd, v, other)], axis=1)
        v = pair.reshape(-1, *v.shape[1:])
    return v


def gather_rest(v, over, *earlier):
    me = lax.axis_index("ctx")
    odd_core, odd_y = (me & 1) == 1, (me >> 1) == 1
    b0, b2, b1, b3 = gather_ctx(v, over, *earlier)
    lo, hi = jnp.where(odd_core, b1, b0), jnp.where(odd_core, b0, b1)
    lo_far, hi_far = jnp.where(odd_core, b3, b2), jnp.where(odd_core, b2, b3)
    whole = jnp.stack(
        [
            jnp.where(odd_y, lo_far, lo),
            jnp.where(odd_y, hi_far, hi),
            jnp.where(odd_y, lo, lo_far),
            jnp.where(odd_y, hi, hi_far),
        ],
        axis=1,
    )
    return whole.reshape(-1, v.shape[2])


def scatter_stages(v, waits):
    n = lax.axis_size("dp")
    me = lax.axis_index("ctx")
    z = lax.axis_index("dp")
    rows, columns = v.shape
    v = v.reshape(n, 2, 2, rows // (4 * n), columns)

    waits = iter(waits)

    def halve(a, i, axis, swap):
        keep = lax.dynamic_index_in_dim(a, i, axis, keepdims=False)
        send = lax.dynamic_index_in_dim(a, 1 - i, axis, keepdims=False)
        other = after(swap(send), *next(waits, []))
        return keep.astype(F32) + other.astype(F32)

    v = halve(v, me & 1, 2, swap_core).astype(BF)
    yield v
    v = halve(v, me >> 1, 1, swap_y)
    bit = 1
    while bit < n:
        v = v.astype(BF)
        yield v
        v = v.reshape(v.shape[0] // 2, 2, *v.shape[1:])
        v = halve(v, (z // bit) & 1, 1, functools.partial(swap_line, bit=bit))
        bit *= 2
    yield v[0]


def sum_stages(v):
    v = v + swap_core(v)
    yield v
    v = v + swap_y(v)
    yield v
    for bit in line_bits():
        v = v + swap_line(v, bit)
        yield v


def attend_kernel(scale, q_ref, k0, k1, k2, k3, *refs):
    o_ref, low_ref, lse_ref = refs[-3:]
    rows = q_ref.shape[0]
    tile = min(QUERY_TILE, rows)
    first = lax.broadcasted_iota(jnp.int32, (1, PAIR), 1) < HD

    def step(i, carry):
        at = pl.ds(pl.multiple_of(i * tile, tile), tile)
        q = q_ref[at, :]
        outs = []
        for h in range(2):
            mine = first if h == 0 else jnp.logical_not(first)
            q_h = jnp.where(mine, q, jnp.zeros_like(q))
            scores = [dot_nt(q_h, k[:, :PAIR]) for k in (k0, k1, k2, k3)]
            top = functools.reduce(
                jnp.maximum, [jnp.max(s, axis=1, keepdims=True) for s in scores]
            )
            acc = None
            for s, k in zip(scores, (k0, k1, k2, k3)):
                p = jnp.exp2((s - top) * scale).astype(BF)
                v = k[:, PAIR:]
                term = dot_nn(p, jnp.where(mine, v, jnp.ones_like(v)))
                acc = term if acc is None else acc + term
            total = pltpu.roll(acc, HD, 1)
            outs.append(acc / total)
            lse = jnp.transpose(top * scale + jnp.log2(total))
            lse_ref[0, pl.ds(h, 1), at] = lse[h * HD : h * HD + 1, :]
        out = jnp.where(first, outs[0], outs[1])
        o_ref[at, :] = out
        low_ref[at, :] = out.astype(BF)
        return carry

    lax.fori_loop(0, rows // tile, step, 0)


def key_specs(rows):
    return [pl.BlockSpec((rows, 2 * PAIR), lambda i: (0, i))] * 4


def attend(q, blocks, call, calls, held, *earlier):
    rows, all_width = q.shape
    width = all_width // calls
    pairs = width // PAIR
    base = call * pairs
    keys = 4 * rows
    spec = pl.BlockSpec((rows, PAIR), lambda i: (0, base + i))
    return pl.pallas_call(
        functools.partial(attend_kernel, LOG2E / math.sqrt(HD)),
        grid=(pairs,),
        in_specs=[spec]
        + key_specs(rows)
        + [pl.BlockSpec(memory_space=pl.ANY)] * (len(held) + len(earlier)),
        out_specs=[spec, spec, pl.BlockSpec((1, 8, rows), lambda i: (base + i, 0, 0))],
        out_shape=[
            jax.ShapeDtypeStruct((rows, all_width), F32),
            jax.ShapeDtypeStruct((rows, all_width), BF),
            jax.ShapeDtypeStruct((calls * pairs, 8, rows), F32),
        ],
        input_output_aliases={5 + i: i for i in range(len(held))},
        cost_estimate=pl.CostEstimate(
            flops=(16 * rows * keys * width) // WEIGHT,
            bytes_accessed=(rows * width * 16) // WEIGHT,
            transcendentals=(rows * keys * width // HD) // WEIGHT,
        ),
        compiler_params=pltpu.CompilerParams(vmem_limit_bytes=VMEM_LIMIT),
        name="attend",
    )(q, *blocks, *held, *earlier)


def attend_back_kernel(scale, factor, blocks, last, q_ref, d_ref, o_ref, lse_ref, *refs):
    rows = q_ref.shape[0]
    keys = 2 * rows
    tile = min(KEY_TILE, rows)
    kv = refs[-2]
    dq_turned = refs[-1]
    dq_ref, out_ref = refs[-4:-2]
    start = 0
    for block in refs[:blocks]:
        kv[start : start + block.shape[0], :] = block[...]
        start += block.shape[0]
    first = lax.broadcasted_iota(jnp.int32, (1, PAIR), 1) < HD
    d = d_ref[...]
    q = q_ref[...]
    prod = jnp.transpose(d.astype(F32) * o_ref[...])
    halves = []
    for h in range(2):
        mine = first if h == 0 else jnp.logical_not(first)
        halves.append((
            jnp.where(mine, q, jnp.zeros_like(q)),
            jnp.where(mine, d, jnp.zeros_like(d)),
            lse_ref[0, h : h + 1, :],
            jnp.sum(prod[h * HD : (h + 1) * HD, :], axis=0, keepdims=True),
        ))
    dq_turned[...] = refs[blocks][...] if last else jnp.zeros_like(dq_turned)

    def step(i, carry):
        at = pl.ds(pl.multiple_of(i * tile, tile), tile)
        k = kv[at, :PAIR]
        v = kv[at, PAIR:]
        k_turned = jnp.transpose(k)
        dk = dv = None
        for h, (q_h, d_h, lse, delta) in enumerate(halves):
            prob = jnp.exp2(dot_nt(k, q_h) * scale - lse)
            d_score = (prob * (dot_nt(v, d_h) - delta)).astype(BF)
            dv_h = dot_nn(prob.astype(BF), d_h)
            dk_h = dot_nn(d_score, q_h)
            dv = dv_h if dv is None else dv + dv_h
            dk = dk_h if dk is None else dk + dk_h
            part = slice(h * HD, (h + 1) * HD)
            dq_turned[part, :] += dot_nn(k_turned[part, :], d_score)
        out_ref[at, :PAIR] = (dk * factor).astype(BF)
        out_ref[at, PAIR:] = dv.astype(BF)
        return carry

    lax.fori_loop(0, keys // tile, step, 0)
    if last:
        dq_ref[...] = (jnp.transpose(dq_turned[...]) * factor).astype(BF)
    else:
        dq_ref[...] = dq_turned[...]


def attend_back(q, d_att, o, lse, blocks, call, partial, *earlier):
    rows = q.shape[0]
    width = blocks[0].shape[1] // 2
    pairs = width // PAIR
    base = call * pairs
    keys = 2 * rows
    last = partial is not None
    wide = pl.BlockSpec((rows, PAIR), lambda i: (0, base + i))
    narrow = pl.BlockSpec((rows, PAIR), lambda i: (0, i))
    turned = pl.BlockSpec((PAIR, rows), lambda i: (i, 0))
    held = [partial] if last else []
    return pl.pallas_call(
        functools.partial(
            attend_back_kernel, LOG2E / math.sqrt(HD), 1.0 / math.sqrt(HD), len(blocks), last
        ),
        grid=(pairs,),
        in_specs=[wide, wide, wide, pl.BlockSpec((1, 8, rows), lambda i: (base + i, 0, 0))]
        + [pl.BlockSpec((b.shape[0], 2 * PAIR), lambda i: (0, i)) for b in blocks]
        + [turned] * len(held)
        + [pl.BlockSpec(memory_space=pl.ANY)] * len(earlier),
        out_specs=[
            narrow if last else turned,
            pl.BlockSpec((keys, 2 * PAIR), lambda i: (0, i)),
        ],
        out_shape=[
            jax.ShapeDtypeStruct((rows, width), BF)
            if last
            else jax.ShapeDtypeStruct((width, rows), F32),
            jax.ShapeDtypeStruct((keys, 2 * width), BF),
        ],
        scratch_shapes=[
            pltpu.VMEM((keys, 2 * PAIR), BF),
            pltpu.VMEM((PAIR, rows), F32),
        ],
        cost_estimate=pl.CostEstimate(
            flops=(40 * rows * keys * width) // WEIGHT,
            bytes_accessed=(rows * width * 40) // WEIGHT,
            transcendentals=(rows * keys * width // HD) // WEIGHT,
        ),
        compiler_params=pltpu.CompilerParams(vmem_limit_bytes=VMEM_LIMIT),
        name="attend_back",
    )(q, d_att, o, lse, *blocks, *held, *earlier)


def mlp_kernel(h2_ref, d_ref, in_ref, down_ref, bias_ref, *refs):
    pair_ref, y_ref, back_ref, bias_grad_ref, y_acc, back_acc = refs[-6:]
    i = pl.program_id(0)
    w_in, w_down = in_ref[...], down_ref[...]
    pre = dot_nn(h2_ref[...], w_in) + bias_ref[...]
    d_act = dot_nn(d_ref[...], w_down)
    below = 0.5 * (1.0 + lax.erf(pre * math.sqrt(0.5)))
    act = (pre * below).astype(BF)
    slope = below + pre * (jnp.exp(-0.5 * pre * pre) * (1.0 / math.sqrt(2.0 * math.pi)))
    d_pre = (d_act * slope).astype(BF)
    pair_ref[0] = d_pre
    pair_ref[1] = act
    bias_grad_ref[...] = jnp.sum(d_pre.astype(F32), axis=0, keepdims=True)
    y = dot_nt(act, w_down)
    back = dot_nt(d_pre, w_in)

    @pl.when(i == 0)
    def _():
        y_acc[...] = y
        back_acc[...] = back

    @pl.when(i > 0)
    def _():
        y_acc[...] += y
        back_acc[...] += back

    @pl.when(i == pl.num_programs(0) - 1)
    def _():
        y_ref[...] = y_acc[...].astype(BF)
        back_ref[...] = back_acc[...].astype(BF)


def mlp(h2, d_down, weights, bias, held, part, parts):
    rows, width = h2.shape
    hidden = bias.shape[1]
    tile = min(HIDDEN_TILE, hidden)
    tiles = hidden // tile
    whole = pl.BlockSpec((rows, width), lambda i: (0, 0))
    mine = pl.BlockSpec((rows, width), lambda i: (part, 0))
    w_in = pl.BlockSpec((width, tile), lambda i: (0, i))
    w_down = pl.BlockSpec((width, tile), lambda i: (0, tiles + i))
    line = pl.BlockSpec((1, tile), lambda i: (0, i))
    more = () if held is None else (held,)
    return pl.pallas_call(
        mlp_kernel,
        grid=(tiles,),
        in_specs=[whole, mine, w_in, w_down, line]
        + [pl.BlockSpec(memory_space=pl.ANY)] * len(more),
        out_specs=[pl.BlockSpec((2, rows, tile), lambda i: (0, part, i)), whole, whole, line],
        out_shape=[
            jax.ShapeDtypeStruct((2, rows * parts, hidden), BF),
            jax.ShapeDtypeStruct((rows, width), BF),
            jax.ShapeDtypeStruct((rows, width), BF),
            jax.ShapeDtypeStruct((1, hidden), F32),
        ],
        scratch_shapes=[pltpu.VMEM((rows, width), F32), pltpu.VMEM((rows, width), F32)],
        input_output_aliases={5: 0} if more else {},
        cost_estimate=pl.CostEstimate(
            flops=(8 * rows * width * hidden) // WEIGHT,
            bytes_accessed=(4 * width * hidden + 4 * rows * hidden + 8 * rows * width) // WEIGHT,
            transcendentals=(rows * hidden) // WEIGHT,
        ),
        compiler_params=pltpu.CompilerParams(vmem_limit_bytes=VMEM_LIMIT),
        name="mlp",
    )(h2, d_down, weights, weights, bias, *more)


def norm_parts(v):
    mean = jnp.mean(v, axis=-1, keepdims=True)
    centred = v - mean
    var = jnp.mean(centred * centred, axis=-1, keepdims=True)
    rstd = lax.rsqrt(var + EPS)
    return centred * rstd, rstd


def norm_back(d, unit, rstd, gain):
    d_unit = d * gain
    return rstd * (
        d_unit
        - jnp.mean(d_unit, axis=-1, keepdims=True)
        - unit * jnp.mean(d_unit * unit, axis=-1, keepdims=True)
    )


def body(
    tokens,
    lengths,
    norm_gain,
    norm_bias,
    qkv_weight,
    qv_bias,
    out_weight,
    mlp_in,
    mlp_bias,
    mlp_out,
    out_bias,
    cotangent,
):
    _, cap, width = tokens.shape
    n_ctx = lax.axis_size("ctx")
    slots = n_ctx * cap
    rows = 3 * slots // 4 // n_ctx
    spare = cap - rows
    local = qkv_weight.shape[2]
    hidden = mlp_in.shape[1]
    share = qkv_weight.shape[0]
    pairs = local // PAIR
    per_call = min(PAIRS_PER_CALL, pairs)
    calls = pairs // per_call
    me = lax.axis_index("ctx")

    small = jnp.concatenate([norm_gain, norm_bias, out_bias], axis=0)
    small = jnp.pad(small.T, ((0, 0), (0, PAIR - small.shape[0])))
    w_kv = jnp.stack(
        [qkv_weight[:, 1].reshape(share, pairs, PAIR), qkv_weight[:, 2].reshape(share, pairs, PAIR)],
        axis=2,
    ).reshape(share, 2 * local)
    tokens_far = swap_y(tokens[0, rows:])
    line = gather_line(jnp.concatenate([qkv_weight[:, 0], w_kv, small], axis=1), tokens_far)
    over = jnp.maximum(lengths - rows, 0)
    lack = jnp.maximum(rows - lengths, 0)
    row = lax.iota(jnp.int32, rows)
    column = lax.iota(jnp.int32, n_ctx * spare)
    owner = (column // spare) ^ me
    slot = column % spare
    my_length = jnp.int32(0)
    my_lack_at = jnp.int32(0)
    source = jnp.full((n_ctx * spare,), -2, jnp.int32)
    over_at = lack_at = jnp.int32(0)
    for c in range(n_ctx):
        my_length = jnp.where(me == c, lengths[c], my_length)
        my_lack_at = jnp.where(me == c, lack_at, my_lack_at)
        source = jnp.where((owner == c) & (slot < over[c]), over_at + slot, source)
        over_at, lack_at = over_at + over[c], lack_at + lack[c]
    own = row < my_length
    need = jnp.where(own, -1, my_lack_at + row - my_length)
    source = source.reshape(n_ctx, spare)
    source = jnp.concatenate([source[0], source[2], source[1], source[3]])
    pick = (need[:, None] == source[None, :]).astype(BF)

    def take(v, over):
        blocks = jnp.concatenate(gather_ctx(v[rows:], over), axis=0)
        return jnp.where(own[:, None], v[:rows], dot_nn(pick, blocks).astype(BF))

    def give_near(v):
        blocks = dot_tn(pick[:, spare:], v).astype(BF)
        return v, blocks, swap_core(blocks[spare:])

    def give_far(v, blocks, got):
        back = swap_y(blocks[:spare] + got[spare:])
        kept = jnp.where(own[:, None], v, jnp.zeros_like(v))
        return jnp.concatenate([kept, got[:spare] + back], axis=0)[None], back

    x_low = take(tokens[0], tokens_far)
    x = x_low.astype(F32)
    unit_one, rstd_one = norm_parts(x)

    line = after(line, x_low)
    line_far = swap_y(line)
    rest = jnp.concatenate([mlp_in, mlp_out.T, out_weight.T], axis=1)
    rest = lax.all_gather(after(rest, line_far), ("dp", "ctx"), axis=0, tiled=True)
    w_out = rest[:, 2 * hidden :]
    first = gather_rest(line, line_far)
    w_q, w_kv, w_qkv = first[:, :local], first[:, local : 3 * local], first[:, : 3 * local]
    small = first[:, 3 * local : 3 * local + 6].T.astype(F32)
    gains, shifts, biases = small[0:2], small[2:4], small[4:6]
    h1 = (unit_one * gains[0] + shifts[0]).astype(BF)
    kv_bias = jnp.stack(
        [jnp.zeros((pairs, PAIR), F32), qv_bias[1].reshape(pairs, PAIR)], axis=1
    ).reshape(2 * local)
    query = (dot_nn(h1, w_q) + qv_bias[0]).astype(BF)
    kvs, far = [], []
    for call in range(calls):
        at = slice(call * per_call * 2 * PAIR, (call + 1) * per_call * 2 * PAIR)
        kvs.append((dot_nn(h1, w_kv[:, at]) + kv_bias[at]).astype(BF))
    held, far, kv_blocks = (), [], []
    for call in range(min(2, calls)):
        kvs[call] = after(kvs[call], *far)
        far.append(swap_y(kvs[call]))
    for call in range(calls):
        kv_blocks.append(gather_ctx(kvs[call], after(far[call], *held[2:])))
        held = attend(query, kv_blocks[call], call, calls, held)
        if call + 2 < calls:
            kvs[call + 2] = after(kvs[call + 2], held[2])
            far.append(swap_y(kvs[call + 2]))
    attn, attended, lse = held
    cot_far = swap_y(after(cotangent[0, rows:], far[-1]))
    d_down = take(cotangent[0], after(cot_far, lse))
    parts = PARTS
    mine = rows // parts
    pair = None
    x_one, y_parts, back_parts, h2, mlp_bias_grad = [], [], [], [], 0.0
    for part in range(parts):
        at = slice(part * mine, (part + 1) * mine)
        branch = sum_tp(dot_nt(attended[at], w_out).astype(BF), *y_parts)
        x_part = x[at] + (branch + biases[0])
        unit, rstd = norm_parts(x_part)
        h2_part = (unit * gains[1] + shifts[1]).astype(BF)
        pair, y_part, back_part, bias_part = mlp(
            h2_part, d_down, rest, mlp_bias[None], pair, part, parts
        )
        x_one.append(x_part)
        h2.append(h2_part)
        y_parts.append(y_part)
        back_parts.append(back_part)
        mlp_bias_grad = mlp_bias_grad + bias_part
    d_h2 = [sum_tp(v, y_parts[-1]) for v in back_parts]
    sides = after(jnp.stack([jnp.concatenate(h2, axis=0), d_down]), *d_h2)
    grads = jnp.einsum("btd,btf->bdf", sides, pair, preferred_element_type=F32).astype(BF)
    grad_mlp = lax.psum_scatter(grads, ("dp", "ctx"), scatter_dimension=1, tiled=True)
    grad_in = grad_mlp[0].astype(F32)
    grad_down = grad_mlp[1].astype(F32).T

    d_x_one, d_att, gain_two, shift_two = [], [], 0.0, 0.0
    for part in range(parts):
        at = slice(part * mine, (part + 1) * mine)
        unit, rstd = norm_parts(x_one[part])
        d_part = d_down[at].astype(F32) + norm_back(d_h2[part], unit, rstd, gains[1])
        d_x_one.append(d_part)
        d_att.append(dot_nn(d_part.astype(BF), w_out).astype(BF))
        gain_two = gain_two + jnp.sum(d_h2[part] * unit, axis=0)
        shift_two = shift_two + jnp.sum(d_h2[part], axis=0)
    d_x_one = jnp.concatenate(d_x_one, axis=0)
    d_att = jnp.concatenate(d_att, axis=0)
    d_branch = d_x_one.astype(BF)
    grad_out = dot_tn(d_branch, attended).astype(BF)
    sums = [
        gain_two,
        shift_two,
        jnp.sum(d_branch.astype(F32), axis=0),
        jnp.sum(d_down.astype(F32), axis=0),
    ]

    d_query, d_kv = [], []
    earlier = [grads]
    result_back = []
    for call in range(calls):
        near, over, *side = kv_blocks[call]
        partial, send = attend_back(query, d_att, attn, lse, side, call, None, *earlier)
        got = swap_core(send)
        dq, keep = attend_back(query, d_att, attn, lse, (near, over), call, partial)
        if call == calls - 1 and call > 2:
            got = after(got, result_back, grad_mlp)
        got = after(got, keep)
        if call == min(1, calls - 1):
            result = give_near(
                jnp.concatenate([
                    (x_part + (sum_tp(after(y_part, d_att), keep) + biases[1])).astype(BF)
                    for x_part, y_part in zip(x_one, y_parts)
                ])
            )
        if call == min(2, calls - 1):
            result, result_back = give_far(*result[:2], after(result[2], keep))
        mid = (keep[rows:].astype(F32) + got[rows:].astype(F32)).astype(BF)
        far_kv = swap_y(mid)
        d_kv.append((keep[:rows], got[:rows], far_kv))
        d_query.append(dq)
        earlier = [mid]
        if call == min(1, calls - 1):
            earlier.append(result[2])
    d_kv = [
        (a.astype(F32) + b.astype(F32) + c.astype(F32)).astype(BF) for a, b, c in d_kv
    ]
    d_qkv = jnp.concatenate(d_query + d_kv, axis=1)
    qkv_sum = jnp.sum(d_qkv.astype(F32), axis=0)
    v_sum = qkv_sum[local:].reshape(pairs, 2, PAIR)[:, 1].reshape(local)
    few = sum_stages(
        jnp.concatenate([qkv_sum[:local], v_sum, mlp_bias_grad[0]]).reshape(-1, PAIR)
    )
    attn_back = dot_nt(d_qkv, w_qkv)
    sums = [jnp.sum(attn_back * unit_one, axis=0), jnp.sum(attn_back, axis=0), *sums]
    sums = jnp.pad(jnp.stack(sums), ((0, PAIR - len(sums)), (0, 0))).T
    grad_attn = jnp.concatenate(
        [dot_tn(h1, d_qkv).astype(BF), grad_out, sums.astype(BF)], axis=1
    )
    attn_low = attn_back.astype(BF)
    waits = [[], [], [], []]
    scatter = scatter_stages(grad_attn, waits)
    next(scatter)
    d_h1 = sum_tp(attn_low, next(scatter))
    grad_rows = (d_x_one + norm_back(d_h1, unit_one, rstd_one, gains[0])).astype(BF)
    rows_back, blocks, got = give_near(grad_rows)
    grad_tokens, tokens_back = give_far(rows_back, blocks, got)
    waits[3].append(tokens_back)
    waits[2].append(grad_rows)
    for few_sums in few:
        pass
    few_sums = few_sums.reshape(-1)
    for grad_attn in scatter:
        pass
    grad_qkv = grad_attn[:, : 3 * local]
    grad_out = grad_attn[:, 3 * local : 4 * local].T
    sums = grad_attn[:, 4 * local : 4 * local + 6].T
    ones = sums[:2]
    if lax.axis_size("tp") == 2:
        ones = ones + lax.ppermute(ones, "tp", [(0, 1), (1, 0)])
    else:
        ones = lax.psum(ones, "tp")
    grad_kv = grad_qkv[:, local:].reshape(share, pairs, 2, PAIR)
    grad_qkv = jnp.stack(
        [
            grad_qkv[:, :local],
            grad_kv[:, :, 0].reshape(share, local),
            grad_kv[:, :, 1].reshape(share, local),
        ],
        axis=1,
    )

    grad_gain = jnp.stack([ones[0], sums[2]])
    grad_shift = jnp.stack([ones[1], sums[3]])
    grad_out_bias = sums[4:6]
    qv_grad = few_sums[: 2 * local].reshape(2, local)
    mlp_bias_sum = few_sums[2 * local :]
    return (
        result,
        grad_tokens,
        grad_gain,
        grad_shift,
        grad_qkv,
        qv_grad,
        grad_out,
        grad_in,
        mlp_bias_sum,
        grad_down,
        grad_out_bias,
    )


def solution(mesh):
    in_specs = (
        P("dp", "ctx", None),
        P(),
        P(None, ("dp", "ctx")),
        P(None, ("dp", "ctx")),
        P(("dp", "ctx"), None, "tp"),
        P(None, "tp"),
        P("tp", ("dp", "ctx")),
        P(("dp", "ctx"), "tp"),
        P("tp"),
        P("tp", ("dp", "ctx")),
        P(None, ("dp", "ctx")),
        P("dp", "ctx", None),
    )
    out_specs = (
        P("dp", "ctx", None),
        P("dp", "ctx", None),
        P(None, ("dp", "ctx")),
        P(None, ("dp", "ctx")),
        P(("dp", "ctx"), None, "tp"),
        P(None, "tp"),
        P("tp", ("dp", "ctx")),
        P(("dp", "ctx"), "tp"),
        P("tp"),
        P("tp", ("dp", "ctx")),
        P(None, ("dp", "ctx")),
    )
    return jax.shard_map(body, mesh=mesh, in_specs=in_specs, out_specs=out_specs, check_vma=False)
```
